128 devices in a mesh: gx: 8 (over x, core), gy: 16 (over z, y).
Axes of the slice: x: 4, y: 4, z: 4, core: 2. Of those that a mesh axis runs over, the one named last changes fastest.
Arguments:
- eta: float32 [16, 1048576], P(None, ('gx', 'gy')), may hold values from -6 to 6
- forcing: float32 [16, 1048576], P(None, ('gx', 'gy')), may hold values from -3 to 3
- couplings: float32 [3, 1048576], P(None, ('gx', 'gy')), may hold values from 0.02 to 0.3
- neighbors: int32 [3, 1048576], P(None, ('gx', 'gy')), may hold values from 0 to 8703, as said below
- halo_send: int32 [128, 512], P(('gx', 'gy')), may hold values from 0 to 8191
- cycle_send: int32 [128, 128, 128], P(('gx', 'gy')), may hold values from 0 to 8191
- stencil: int32 [3, 2097152], P(None, ('gx', 'gy')), may hold values from 0 to 16383
- stencil_weights: float32 [3, 2097152], P(None, ('gx', 'gy')), as said below
- m_order: int32 [1024], replicated, may hold values from 0 to 1023, as said below
- lat_weights: float32 [1024], replicated, may hold values from 0.5 to 1.5
- love: float32 [1024], replicated, may hold values from 0.1 to 2
- legendre: bfloat16 [1024, 1024, 1024], P(('gx', 'gy')), as said below
Outputs:
- stepped: float32 [16, 1048576], P(None, ('gx', 'gy'))
- loading: float32 [16, 1048576], P(None, ('gx', 'gy'))
The draws below stay inside these ranges and needn't reach their ends.
Inputs may be any that keep to these rules, and one draw needn't show every extreme that they name: `neighbors`: positions below 8192 are the partition's own cells, the rest its halo cells. `m_order`: each order appears once. legendre[j, l, :] is zero for l < m_order[j]. `stencil_weights`: the 3 weights of a grid point are positive and sum to one.
All inputs are finite; a program needn't handle non-finite values.
Results may differ from the reference program's by a relative error of at most 0.0044.
Values may be sent and summed in bfloat16 or wider, within the bound.
A program may use at most 128 MiB of HBM per device.

```python
import math
import jax
import jax.numpy as jnp
from jax import lax

NF = 16
CELLS_DEV = 8192
NB = 3
NLAT = 1024
NLON = 2048
DEG = 1024
BAND = 128
HALO = 256
CAP = 128
CELLS = 1048576
SLOTS = 16384
CYCLES_DEV = 8
N_GX = 8
N_GY = 16


def order_of(key):
    return jax.random.permutation(jax.random.fold_in(key, 11), DEG).astype(jnp.int32)


def draw_m_order(key, part):
    return order_of(key)


def draw_legendre(key, part):
    order = order_of(key)
    degrees = jnp.arange(DEG, dtype=jnp.int32)
    table_key = jax.random.fold_in(key, 12)

    def one_slot(slot):
        slot_key = jax.random.fold_in(table_key, slot)
        values = jax.random.normal(slot_key, (DEG, NLAT), jnp.float32) / math.sqrt(NLAT)
        live = (degrees >= order[slot]).astype(jnp.float32)
        return (values * live[:, None]).astype(jnp.bfloat16)
    return lax.map(one_slot, jnp.arange(DEG, dtype=jnp.int32))


def draw_neighbors(key, part):
    first, second, third = jax.random.split(key, 3)
    inner = jax.random.randint(first, (NB, CELLS), 0, CELLS_DEV, dtype=jnp.int32)
    outer = jax.random.randint(second, (NB, CELLS), CELLS_DEV, CELLS_DEV + 2 * HALO, dtype=jnp.int32)
    picks = jax.random.randint(third, (NB, CELLS), 0, 8, dtype=jnp.int32)
    chosen = jnp.where(picks == 0, outer, inner)
    return chosen.at[0, 0].set(CELLS_DEV + 2 * HALO - 1)


def draw_stencil_weights(key, part):
    raw = jax.random.uniform(key, (NB, NLAT * NLON), jnp.float32, 0.1, 1.0)
    return raw / jnp.sum(raw, axis=0, keepdims=True)


def touch_ends(entries, stream_key, smallest, high):
    shape = entries.shape
    index_at = [jax.random.randint(jax.random.fold_in(stream_key, axis), (), 0, shape[axis]) for axis in range(len(shape))]
    entries = entries.at[tuple(index_at)].set(smallest)
    longest = shape.index(max(shape))
    index_at[longest] = (index_at[longest] + 1) % shape[longest]
    return entries.at[tuple(index_at)].set(high)


def levels(own_key, extent, cuts, smallest, largest):
    loudness = 1.0
    for dim, parts in cuts:
        draws = jax.random.uniform(jax.random.fold_in(jax.random.fold_in(own_key, 6), dim), (parts,), jnp.float32, smallest / len(cuts), largest / len(cuts))
        loudness = loudness * jnp.repeat(jnp.exp(draws), extent[dim] // parts).reshape((-1,) + (1,) * (len(extent) - 1 - dim))
    return loudness


def normal_values(key, dims, scale, limit, cuts=(), kind=jnp.bfloat16):
    drawn = scale * jax.random.normal(key, dims, jnp.float32)
    if cuts:
        drawn = drawn * levels(key, dims, cuts, -0.22, 0.18)
    return jnp.clip(drawn, -limit, limit).astype(kind)


def setup_inputs(seed: int = 0) -> dict:
    seeds = jax.random.split(jax.random.key(seed), 13)
    return {
        "eta": normal_values(seeds[0], (NF, CELLS), 1.0, 6.0, ((1, 128),), jnp.float32),
        "forcing": normal_values(seeds[1], (NF, CELLS), 0.5, 3.0, ((1, 128),), jnp.float32),
        "couplings": jnp.clip(jnp.exp(math.log(0.3) - 2.7080503 * jax.random.uniform(seeds[2], (NB, CELLS), jnp.float32) ** levels(seeds[2], (NB, CELLS), ((1, 128),), -0.2, 0.2)), 0.02, 0.3),
        "neighbors": draw_neighbors(jax.random.fold_in(seeds[12], 71), 0),
        "halo_send": touch_ends(jax.random.randint(seeds[4], (N_GX * N_GY, 2 * HALO), 0, CELLS_DEV), jax.random.fold_in(seeds[4], 1), 0, CELLS_DEV - 1).astype(jnp.int32),
        "cycle_send": touch_ends(jax.random.randint(seeds[5], (N_GX * N_GY, BAND, CAP), 0, CELLS_DEV), jax.random.fold_in(seeds[5], 1), 0, CELLS_DEV - 1).astype(jnp.int32),
        "stencil": touch_ends(jax.random.randint(seeds[6], (NB, NLAT * NLON), 0, SLOTS), jax.random.fold_in(seeds[6], 1), 0, SLOTS - 1).astype(jnp.int32),
        "stencil_weights": draw_stencil_weights(jax.random.fold_in(seeds[12], 71), 0),
        "m_order": draw_m_order(jax.random.fold_in(seeds[12], 71), 0),
        "lat_weights": jnp.clip(jax.random.uniform(seeds[9], (NLAT,), jnp.float32, 0.5, 1.5), 0.5, 1.5),
        "love": jnp.clip(jnp.exp(jax.random.uniform(seeds[10], (DEG,), jnp.float32, math.log(0.1), math.log(2.0))), 0.1, 2.0),
        "legendre": draw_legendre(jax.random.fold_in(seeds[12], 71), 0),
    }


def wave_tables(m_order, points_count):
    points = jnp.arange(points_count, dtype=jnp.int32)
    phase = (points[:, None] * m_order[None, :].astype(jnp.int32)) % points_count
    angle = phase.astype(jnp.float32) * (2.0 * math.pi / points_count)
    return jnp.cos(angle), jnp.sin(angle)


def reference(eta, forcing, couplings, neighbors, halo_send, cycle_send, stencil, stencil_weights, m_order, lat_weights, love, legendre):
    partitions = N_GX * N_GY
    fields = eta.shape[0]
    rim_width = HALO
    slot_count = CAP
    points = CYCLES_DEV * NLON
    cells_now = eta.reshape(fields, partitions, CELLS_DEV)
    rim_index = jnp.broadcast_to(halo_send.reshape(1, partitions, 2 * rim_width), (fields, partitions, 2 * rim_width))
    rim_values = jnp.take_along_axis(cells_now, rim_index, axis=2)
    from_lower = jnp.roll(rim_values, 1, axis=1)[:, :, rim_width:]
    from_upper = jnp.roll(rim_values, -1, axis=1)[:, :, :rim_width]
    extended = jnp.concatenate([cells_now, from_lower, from_upper], axis=2)
    neighbor_index = neighbors.reshape(NB, partitions, CELLS_DEV)
    coupling = couplings.reshape(NB, partitions, CELLS_DEV)
    change = jnp.zeros(cells_now.shape, jnp.float32)
    for which in range(NB):
        values = jnp.take_along_axis(extended, jnp.broadcast_to(neighbor_index[which][None], cells_now.shape), axis=2)
        change = change + coupling[which][None] * (values - cells_now)
    stepped = cells_now + change + forcing.reshape(fields, partitions, CELLS_DEV)
    send_index = jnp.broadcast_to(cycle_send.reshape(1, partitions, BAND * slot_count), (fields, partitions, BAND * slot_count))
    outgoing = jnp.take_along_axis(stepped, send_index, axis=2).reshape(fields, partitions, BAND, slot_count)
    incoming = jnp.transpose(outgoing, (0, 2, 1, 3)).reshape(fields, BAND, partitions * slot_count)
    stencil_index = stencil.reshape(NB, partitions, points)
    stencil_wts = stencil_weights.reshape(NB, partitions, points)
    gridded = jnp.zeros((fields, partitions, points), jnp.float32)
    for which in range(NB):
        picked = jnp.take_along_axis(incoming, jnp.broadcast_to(stencil_index[which][None], (fields, partitions, points)), axis=2)
        gridded = gridded + stencil_wts[which][None] * picked
    cosines, sines = wave_tables(m_order, NLON)
    scale = NLON ** -0.5
    flat = gridded.reshape(fields * NLAT, NLON)
    cosine_part = jnp.dot(flat, cosines, precision=lax.Precision.HIGHEST, preferred_element_type=jnp.float32) * scale
    sine_part = jnp.dot(flat, sines, precision=lax.Precision.HIGHEST, preferred_element_type=jnp.float32) * scale
    fourier = jnp.stack([cosine_part, sine_part]).astype(jnp.bfloat16).reshape(2 * fields, NLAT, DEG)
    by_order = jnp.transpose(fourier, (2, 0, 1))

    def one_order(pair):
        spectra, legendre_rows = pair
        weighted = (spectra.astype(jnp.float32) * lat_weights[None, :]).astype(jnp.bfloat16)
        coefficients = jnp.dot(weighted, legendre_rows.T, preferred_element_type=jnp.float32)
        scaled = (coefficients * love[None, :]).astype(jnp.bfloat16)
        return jnp.dot(scaled, legendre_rows, preferred_element_type=jnp.float32).astype(jnp.bfloat16)

    synthesized = lax.map(one_order, (by_order, legendre))
    spectral = jnp.transpose(synthesized, (1, 2, 0)).astype(jnp.float32).reshape(2, fields * NLAT, DEG)
    returned_grid = jnp.dot(spectral[0], cosines.T, precision=lax.Precision.HIGHEST, preferred_element_type=jnp.float32)
    returned_grid = returned_grid + jnp.dot(spectral[1], sines.T, precision=lax.Precision.HIGHEST, preferred_element_type=jnp.float32)
    returned_grid = (returned_grid * scale).reshape(fields, partitions, points)

    def spread(index_rows, weight_rows, values):
        total = jnp.zeros((fields, partitions * slot_count), jnp.float32)
        for which in range(NB):
            total = total.at[:, index_rows[which]].add(weight_rows[which][None, :] * values)
        return total

    slot_sums = jax.vmap(spread, in_axes=(1, 1, 1))(stencil_index, stencil_wts, returned_grid)
    slot_sums = slot_sums.reshape(BAND, fields, partitions, slot_count)
    toward_cells = jnp.transpose(slot_sums, (2, 1, 0, 3)).reshape(partitions, fields, BAND * slot_count)

    def gather_home(index_row, values):
        return jnp.zeros((fields, CELLS_DEV), jnp.float32).at[:, index_row].add(values)

    loading = jax.vmap(gather_home)(cycle_send.reshape(partitions, BAND * slot_count), toward_cells)
    loading = jnp.transpose(loading, (1, 0, 2)).reshape(fields, partitions * CELLS_DEV)
    return stepped.reshape(fields, partitions * CELLS_DEV), loading
```

```python
import functools
import math

import jax
import jax.numpy as jnp
import numpy as np
from jax import lax
from jax.experimental import pallas as pl
from jax.experimental.pallas import tpu as pltpu
from jax.sharding import PartitionSpec as P

BF = jnp.bfloat16
F32 = jnp.float32
I32 = jnp.int32
F = 16
W = 256
NT = (((1,), (1,)), ((), ()))


def lane_one_hot(row):
    n = row.shape[1]
    return jnp.where(lax.broadcasted_iota(I32, (W, n), 0) == (row & (W - 1)), 1.0, 0.0).astype(BF)


def gather(table, row):
    n = row.shape[1]
    picked = jnp.dot(table, lane_one_hot(row), preferred_element_type=F32)
    group = jnp.broadcast_to(row >> 8, (F, n))
    out = picked[:F]
    for g in range(1, table.shape[0] // F):
        out = jnp.where(group == g, picked[g * F : (g + 1) * F], out)
    return out


def spread(values, row, groups):
    n = row.shape[1]
    group = jnp.broadcast_to((row >> 8).astype(F32), (F, n)).astype(BF)
    return jnp.concatenate(
        [jnp.where(group == BF(g), values, BF(0)) for g in range(groups)], axis=0
    )


def aligned(start, step):
    return pl.multiple_of(start, step)


def index_row(ref, block, rows):
    part = ref[0, pl.ds(aligned(block * rows, rows), rows), :]
    return jnp.concatenate([part[r : r + 1] for r in range(rows)], axis=1)


def halo_kernel(eta_ref, send_ref, low_ref, high_ref):
    table = jnp.concatenate(
        [eta_ref[:, g * W : (g + 1) * W].astype(BF) for g in range(32)], axis=0
    )
    rim = gather(table, send_ref[...]).astype(BF)
    low_ref[...] = rim[:, :W]
    high_ref[...] = rim[:, W:]


def step_kernel(
    eta_ref, forcing_ref, coup_ref, nbr_ref, below_ref, above_ref, send_ref,
    stepped_ref, out_ref, table, table2,
):
    for g in range(32):
        table[g * F : (g + 1) * F] = eta_ref[:, g * W : (g + 1) * W].astype(BF)
    table[32 * F : 33 * F] = below_ref[...]
    table[33 * F : 34 * F] = above_ref[...]

    def step(b, carry):
        at = pl.ds(aligned(b * 512, 512), 512)
        here = eta_ref[:, at]
        total = here + forcing_ref[:, at]
        for k in range(3):
            total += coup_ref[k : k + 1, at] * (gather(table[...], nbr_ref[k : k + 1, at]) - here)
        stepped_ref[:, at] = total
        rounded = total.astype(BF)
        table2[pl.ds(aligned(b * 32, 32), F)] = rounded[:, :W]
        table2[pl.ds(aligned(b * 32 + F, F), F)] = rounded[:, W:]
        return carry

    lax.fori_loop(0, 16, step, 0)

    def send(b, carry):
        row = index_row(send_ref, b, 8)
        for half in range(2):
            got = gather(table2[...], row[:, half * 512 : half * 512 + 512]).astype(BF)
            for r in range(4):
                out_ref[b * 8 + half * 4 + r] = got[:, r * 128 : r * 128 + 128]
        return carry

    lax.fori_loop(0, 16, send, 0)


def order_slot(row):
    return (row & 1) * 512 + (row >> 1)


def grid_kernel(
    in_ref, sten_ref, wts_ref, m_ref, wave_hbm, wave_lo_hbm, out_ref,
    table, grid, wave, wave_lo, sems,
):
    copies = [
        pltpu.make_async_copy(wave_hbm, wave, sems.at[0]),
        pltpu.make_async_copy(wave_lo_hbm, wave_lo, sems.at[1]),
    ]
    for c in copies:
        c.start()
    for g in range(64):
        table[g * F : (g + 1) * F, :128] = in_ref[2 * g]
        table[g * F : (g + 1) * F, 128:] = in_ref[2 * g + 1]

    def pick(b, carry):
        at = pl.ds(aligned(b * 512, 512), 512)
        total = jnp.zeros((F, 512), F32)
        for k in range(3):
            total += gather(table[...], sten_ref[k : k + 1, at]) * wts_ref[k : k + 1, at]
        grid[pl.ds(aligned(b // 4 * F, F), F), pl.ds(aligned(b % 4 * 512, 512), 512)] = total
        return carry

    lax.fori_loop(0, 32, pick, 0)
    for c in copies:
        c.wait()
    scale = 2048.0**-0.5
    parts = []
    for parity in range(2):
        near, far = grid[:, :1024], grid[:, 1024:]
        folded = near + far if parity == 0 else near - far
        high = folded.astype(BF)
        low = (folded - high.astype(F32)).astype(BF)
        both = jnp.concatenate([high, low], axis=0)
        first = lax.dot_general(wave[parity], both, NT, preferred_element_type=F32)
        second = lax.dot_general(wave_lo[parity], high, NT, preferred_element_type=F32)
        parts.append(((first[:, :128] + first[:, 128:] + second) * scale).astype(BF))
    slot = jnp.broadcast_to(order_slot(m_ref[...]).astype(F32), (128, 1024))
    column = jnp.concatenate(
        [slot[:, r * 128 : r * 128 + 128].T for r in range(8)], axis=0
    ).astype(I32)
    lane = lax.broadcasted_iota(I32, (1024, 128), 1)
    chosen = jnp.concatenate(
        [jnp.where(column == lane + r * 128, 1.0, 0.0).astype(BF) for r in range(8)], axis=1
    )
    rows = []
    for c in range(2):
        source = jnp.concatenate([parts[0][c * 512 : c * 512 + 512], parts[1][c * 512 : c * 512 + 512]], axis=0)
        rows.append(jnp.dot(chosen, source, preferred_element_type=F32).reshape(128, 8, 128))
    out_ref[...] = jnp.concatenate(rows, axis=1).astype(BF)


def order_kernel(in_ref, lat_ref, love_ref, leg_ref, out_ref, wide, left, right):
    j = pl.program_id(0)

    def shuffle(flip):
        a = lax.broadcasted_iota(I32, (1024, 1024), 1 if flip else 0)
        b = lax.broadcasted_iota(I32, (1024, 1024), 0 if flip else 1)
        return jnp.where((b >> 3) + (b & 7) * 128 == a, 1.0, 0.0).astype(BF)

    @pl.when(j == 0)
    def _():
        wide[...] = in_ref[...].astype(F32).reshape(2048, 128)
        blocks = []
        for o in range(8):
            for c in range(2):
                turned = wide[pl.ds(c * 8 + o, 128, stride=16), :].T
                blocks.append(
                    jnp.concatenate([turned[i * F : (i + 1) * F] for i in range(8)], axis=1)
                )
        spectra = jnp.dot(
            jnp.concatenate(blocks, axis=0).astype(BF), shuffle(False), preferred_element_type=F32
        )
        left[...] = (spectra * lat_ref[...]).astype(BF)

    at = pl.ds(aligned(j * 32, 32), 32)
    legendre = leg_ref[0]
    coefficients = lax.dot_general(left[at], legendre, NT, preferred_element_type=F32)
    scaled = (coefficients * love_ref[...]).astype(BF)
    right[at] = jnp.dot(scaled, legendre, preferred_element_type=F32).astype(BF)

    @pl.when(j == 7)
    def _():
        back = jnp.dot(right[...], shuffle(True), preferred_element_type=F32)
        for o in range(8):
            for c in range(2):
                block = back[(o * 2 + c) * F : (o * 2 + c + 1) * F]
                turned = jnp.concatenate(
                    [block[:, i * 128 : i * 128 + 128] for i in range(8)], axis=0
                ).T
                wide[pl.ds(c * 8 + o, 128, stride=16), :] = turned
        out_ref[...] = wide[...].reshape(128, 16, 128).astype(BF)


def slot_kernel(
    in_ref, sten_ref, wts_ref, m_ref, wave_hbm, wave_lo_hbm, out_ref,
    grid, sums, wave, wave_lo, sems,
):
    copies = [
        pltpu.make_async_copy(wave_hbm, wave, sems.at[0]),
        pltpu.make_async_copy(wave_lo_hbm, wave_lo, sems.at[1]),
    ]
    for c in copies:
        c.start()
    arrived = in_ref[...].astype(F32)
    slot = order_slot(m_ref[...])
    chosen = jnp.where(lax.broadcasted_iota(I32, (1024, 1024), 0) == slot, 1.0, 0.0).astype(BF)
    turned = []
    for c in range(2):
        rows = arrived[:, c * 8 : c * 8 + 8].reshape(1024, 128).astype(BF)
        placed = jnp.dot(chosen, rows, preferred_element_type=F32)
        turned.append(
            jnp.concatenate([placed[r * 128 : r * 128 + 128].T for r in range(8)], axis=1).astype(BF)
        )
    for c in copies:
        c.wait()
    sides = []
    for parity in range(2):
        at = slice(parity * 512, parity * 512 + 512)
        source = jnp.concatenate([turned[0][:, at], turned[1][:, at]], axis=1)
        sides.append(
            jnp.dot(source, wave[parity], preferred_element_type=F32)
            + jnp.dot(source, wave_lo[parity], preferred_element_type=F32)
        )
    scale = 2048.0**-0.5
    grid[:, :1024] = (sides[0] + sides[1]) * scale
    grid[:, 1024:] = (sides[0] - sides[1]) * scale
    sums[...] = jnp.zeros_like(sums)

    def add(b, carry):
        at = pl.ds(aligned(b * 1024, 1024), 1024)
        here = grid[pl.ds(aligned(b // 2 * F, F), F), pl.ds(aligned(b % 2 * 1024, 1024), 1024)]
        left, right = [], []
        for k in range(3):
            row = sten_ref[k : k + 1, at]
            left.append(spread((here * wts_ref[k : k + 1, at]).astype(BF), row, 64))
            right.append(lane_one_hot(row))
        sums[...] += lax.dot_general(
            jnp.concatenate(left, axis=1), jnp.concatenate(right, axis=1), NT,
            preferred_element_type=F32,
        )
        return carry

    lax.fori_loop(0, 16, add, 0)
    for g in range(64):
        out_ref[2 * g] = sums[g * F : (g + 1) * F, :128].astype(BF)
        out_ref[2 * g + 1] = sums[g * F : (g + 1) * F, 128:].astype(BF)


def home_kernel(in_ref, send_ref, out_ref, sums):
    sums[...] = jnp.zeros_like(sums)

    def add(b, carry):
        row = index_row(send_ref, b, 8)
        values = jnp.concatenate([in_ref[b * 8 + r] for r in range(8)], axis=1)
        sums[...] += lax.dot_general(
            spread(values, row, 32), lane_one_hot(row), NT, preferred_element_type=F32
        )
        return carry

    lax.fori_loop(0, 16, add, 0)
    for g in range(32):
        out_ref[:, g * W : (g + 1) * W] = sums[g * F : (g + 1) * F]


VM = pl.BlockSpec(memory_space=pltpu.VMEM)
ANY = pl.BlockSpec(memory_space=pl.ANY)


def call(kernel, out_shape, in_specs, scratch, *args):
    return pl.pallas_call(
        kernel,
        out_shape=out_shape,
        in_specs=in_specs,
        out_specs=jax.tree.map(lambda _: VM, out_shape),
        scratch_shapes=scratch,
        compiler_params=pltpu.CompilerParams(vmem_limit_bytes=56 << 20),
    )(*args)


def shape(dims, kind=BF):
    return jax.ShapeDtypeStruct(dims, kind)


def waves():
    m = np.arange(1024)
    n = np.arange(1024)
    angle = 2.0 * math.pi * ((m[:, None] * n[None, :]) % 2048) / 2048.0
    table = np.stack([np.cos(angle), np.sin(angle)])
    table = np.stack([table[:, p::2].reshape(1024, 1024) for p in range(2)])
    high = table.astype(BF)
    return high, (table - high.astype(np.float64)).astype(BF)


AXES = ("gx", "gy")
PACK = (128, F, 128)


def exchange(blocks):
    return lax.all_to_all(blocks, AXES, split_axis=0, concat_axis=0, tiled=True)


def on_device(
    eta, forcing, couplings, neighbors, halo_send, cycle_send, stencil, stencil_weights,
    m_order, lat_weights, love, legendre,
):
    parts = lax.axis_size("gx") * lax.axis_size("gy")
    m_row = m_order.reshape(1, -1)
    wave, wave_lo = (jnp.asarray(t) for t in waves())
    low, high = call(halo_kernel, (shape((F, W)), shape((F, W))), [VM] * 2, [], eta, halo_send)
    below = lax.ppermute(high, AXES, [(i, (i + 1) % parts) for i in range(parts)])
    above = lax.ppermute(low, AXES, [((i + 1) % parts, i) for i in range(parts)])
    stepped, leaving = call(
        step_kernel, (shape(eta.shape, F32), shape(PACK)), [VM] * 7,
        [pltpu.VMEM((34 * F, W), BF), pltpu.VMEM((32 * F, W), BF)],
        eta, forcing, couplings, neighbors, below, above, cycle_send,
    )
    incoming = exchange(leaving)
    wave_scratch = [
        pltpu.VMEM((2, 1024, 1024), BF), pltpu.VMEM((2, 1024, 1024), BF),
        pltpu.SemaphoreType.DMA((2,)),
    ]
    fourier = call(
        grid_kernel, shape(PACK), [VM] * 4 + [ANY] * 2,
        [pltpu.VMEM((64 * F, W), BF), pltpu.VMEM((128, 2048), F32)] + wave_scratch,
        incoming, stencil, stencil_weights, m_row, wave, wave_lo,
    )
    spectra = exchange(fourier)
    whole = lambda *dims: pl.BlockSpec(dims, lambda j: (0,) * len(dims))
    synthesized = pl.pallas_call(
        order_kernel,
        out_shape=shape(PACK),
        grid=(8,),
        in_specs=[
            whole(*PACK), whole(1, 1024), whole(1, 1024),
            pl.BlockSpec((1, 1024, 1024), lambda j: (j, 0, 0)),
        ],
        out_specs=whole(*PACK),
        scratch_shapes=[
            pltpu.VMEM((2048, 128), F32), pltpu.VMEM((256, 1024), BF), pltpu.VMEM((256, 1024), BF),
        ],
        compiler_params=pltpu.CompilerParams(vmem_limit_bytes=56 << 20),
    )(spectra, lat_weights.reshape(1, -1), love.reshape(1, -1), legendre)
    returned = exchange(synthesized)
    slots = call(
        slot_kernel, shape(PACK), [VM] * 4 + [ANY] * 2,
        [pltpu.VMEM((128, 2048), F32), pltpu.VMEM((64 * F, W), F32)] + wave_scratch,
        returned, stencil, stencil_weights, m_row, wave, wave_lo,
    )
    homeward = exchange(slots)
    loading = call(
        home_kernel, shape(eta.shape, F32), [VM] * 2, [pltpu.VMEM((32 * F, W), F32)],
        homeward, cycle_send,
    )
    return stepped, loading


def solution(mesh):
    both = ("gx", "gy")
    cells = P(None, both)
    placed = (
        cells, cells, cells, cells, P(both, None), P(both, None, None), cells, cells,
        P(), P(), P(), P(both, None, None),
    )
    return jax.shard_map(
        on_device, mesh=mesh, in_specs=placed, out_specs=(cells, cells), check_vma=False
    )
```

```python
import functools
import math

import jax
import jax.numpy as jnp
import numpy as np
from jax import lax
from jax.experimental import pallas as pl
from jax.experimental.pallas import tpu as pltpu
from jax.sharding import PartitionSpec as P

BF = jnp.bfloat16
F32 = jnp.float32
I32 = jnp.int32
F = 16
W = 256
NT = (((1,), (1,)), ((), ()))
MESH = pl.DeviceIdType.MESH
AXES = ("gx", "gy")
PARTS = 128
PACK = (PARTS, F, 128)
SCALE = 2048.0**-0.5


def place(part):
    return (part // 16, lax.rem(part, 16))


def later(part, steps):
    return lax.rem(part + steps, PARTS)


class Exchange:
    def __init__(self, me, out, into, send_sem, recv_sems, group=PARTS):
        self.me, self.out, self.into = me, out, into
        self.send_sem, self.recv_sems, self.group = send_sem, recv_sems, group

    def send(self, steps):
        to = later(self.me, steps)
        pltpu.make_async_remote_copy(
            src_ref=self.out.at[to],
            dst_ref=self.into.at[self.me],
            send_sem=self.send_sem,
            recv_sem=self.recv_sems.at[steps // self.group],
            device_id=place(to),
            device_id_type=MESH,
        ).start()

    def keep(self):
        self.into[self.me] = self.out[self.me]

    def send_all(self):
        def one(steps, carry):
            self.send(steps)
            return carry

        lax.fori_loop(1, PARTS, one, 0)
        self.keep()

    def tiles(self, count, sem):
        at = pl.ds(0, count)
        return pltpu.make_async_remote_copy(
            src_ref=self.out.at[at],
            dst_ref=self.into.at[at],
            send_sem=self.send_sem,
            recv_sem=self.recv_sems.at[sem],
            device_id=place(later(self.me, 1)),
            device_id_type=MESH,
        )

    def wait_group(self, group, count):
        self.tiles(count, group).wait_recv()

    def wait_sent(self):
        self.tiles(PARTS - 1, 0).wait_send()


def lane_one_hot(row):
    n = row.shape[1]
    return jnp.where(lax.broadcasted_iota(I32, (W, n), 0) == (row & (W - 1)), 1.0, 0.0).astype(BF)


def gather(table, row):
    n = row.shape[1]
    picked = jnp.dot(table, lane_one_hot(row), preferred_element_type=F32)
    group = jnp.broadcast_to(row >> 8, (F, n))
    out = picked[:F]
    for g in range(1, table.shape[0] // F):
        out = jnp.where(group == g, picked[g * F : (g + 1) * F], out)
    return out


def spread(values, row, groups):
    n = row.shape[1]
    group = jnp.broadcast_to((row >> 8).astype(F32), (F, n)).astype(BF)
    return jnp.concatenate(
        [jnp.where(group == BF(g), values, BF(0)) for g in range(groups)], axis=0
    )


def aligned(start, step):
    return pl.multiple_of(start, step)


def order_slot(row):
    return (row & 1) * 512 + (row >> 1)


def kernel(
    eta_ref, forcing_ref, coup_ref, nbr_ref, halo_ref, send_ref, sten_hbm, wts_hbm, m_ref, lat_ref,
    love_ref, leg_hbm, wave_hbm, wave_lo_hbm,
    stepped_ref, loading_ref,
    table, table2, rim, slots, grid, wide, left, right, sums, cell_sums, chosen, chosen_t, mix, mix_t,
    sten_ref, wts_ref, leg, wave, wave_lo,
    out0, in0, out1, in1, out2, in2, out3, in3,
    load_sems, leg_sems, halo_send, halo_recv, send_sems, recv0, recv1, recv2, recv3,
):
    me = lax.axis_index("gx") * 16 + lax.axis_index("gy")
    barrier = pltpu.get_barrier_semaphore()

    def greet(steps, carry):
        pl.semaphore_signal(barrier, inc=1, device_id=place(later(me, steps)), device_id_type=MESH)
        return carry

    lax.fori_loop(1, PARTS, greet, 0)
    loads = [
        pltpu.make_async_copy(src, dst, load_sems.at[i])
        for i, (src, dst) in enumerate(
            [(sten_hbm, sten_ref), (wts_hbm, wts_ref), (wave_hbm, wave), (wave_lo_hbm, wave_lo)]
        )
    ]
    leg_loads = [pltpu.make_async_copy(leg_hbm.at[o], leg.at[o], leg_sems.at[o]) for o in range(8)]
    for load in loads + leg_loads:
        load.start()

    for g in range(32):
        table[g * F : (g + 1) * F] = eta_ref[:, g * W : (g + 1) * W].astype(BF)
    rim[...] = gather(table[: 32 * F], halo_ref[...]).astype(BF)
    slot = order_slot(m_ref[...])
    for r in range(8):
        at = slice(r * 128, r * 128 + 128)
        row = lax.broadcasted_iota(I32, (128, 1024), 0) + r * 128
        lane = lax.broadcasted_iota(I32, (128, 1024), 1)
        chosen[at] = jnp.where(slot == row, 1.0, 0.0).astype(BF)
        column = jnp.broadcast_to(slot[:, at].astype(F32), (128, 128)).T.astype(I32)
        for s in range(8):
            side = slice(s * 128, s * 128 + 128)
            chosen_t[at, side] = jnp.where(column == lane[:, side], 1.0, 0.0).astype(BF)
        mix[at] = jnp.where((lane >> 3) + (lane & 7) * 128 == row, 1.0, 0.0).astype(BF)
        mix_t[at] = jnp.where((row >> 3) + (row & 7) * 128 == lane, 1.0, 0.0).astype(BF)

    pl.semaphore_wait(barrier, PARTS - 1)
    halos = []
    for i, (start, to) in enumerate([(W, later(me, 1)), (0, later(me, PARTS - 1))]):
        halos.append(
            pltpu.make_async_remote_copy(
                src_ref=rim.at[:, pl.ds(start, W)],
                dst_ref=table.at[pl.ds((32 + i) * F, F)],
                send_sem=halo_send.at[i],
                recv_sem=halo_recv.at[i],
                device_id=place(to),
                device_id_type=MESH,
            )
        )
    for halo in halos:
        halo.start()
    for halo in halos:
        halo.wait()

    def step(b, carry):
        at = pl.ds(aligned(b * 512, 512), 512)
        here = eta_ref[:, at]
        total = here + forcing_ref[:, at]
        for k in range(3):
            total += coup_ref[k : k + 1, at] * (gather(table[...], nbr_ref[k : k + 1, at]) - here)
        stepped_ref[:, at] = total
        rounded = total.astype(BF)
        table2[pl.ds(aligned(b * 32, 32), F)] = rounded[:, :W]
        table2[pl.ds(aligned(b * 32 + F, F), F)] = rounded[:, W:]
        return carry

    lax.fori_loop(0, 16, step, 0)

    cells = Exchange(me, out0, in0, send_sems.at[0], recv0)

    def send(b, carry):
        for half in range(2):
            steps = [b * 8 + half * 4 + r for r in range(4)]
            row = jnp.concatenate([send_ref[0, pl.ds(later(me, s), 1), :] for s in steps], axis=1)
            got = gather(table2[...], row).astype(BF)
            for r in range(4):
                out0[later(me, steps[r])] = got[:, r * 128 : r * 128 + 128]
                if half + r == 0:
                    pl.when(b > 0)(functools.partial(cells.send, steps[r]))
                else:
                    cells.send(steps[r])
        return carry

    lax.fori_loop(0, 16, send, 0)
    cells.keep()
    for load in loads:
        load.wait()
    cells.wait_group(0, PARTS - 1)
    for g in range(64):
        slots[g * F : (g + 1) * F, :128] = in0[2 * g]
        slots[g * F : (g + 1) * F, 128:] = in0[2 * g + 1]

    def pick(b, carry):
        at = pl.ds(aligned(b * 512, 512), 512)
        total = jnp.zeros((F, 512), F32)
        for k in range(3):
            total += gather(slots[...], sten_ref[k : k + 1, at]) * wts_ref[k : k + 1, at]
        grid[pl.ds(aligned(b // 4 * F, F), F), pl.ds(aligned(b % 4 * 512, 512), 512)] = total
        return carry

    lax.fori_loop(0, 32, pick, 0)

    halves = []
    for parity in range(2):
        near, far = grid[:, :1024], grid[:, 1024:]
        folded = near + far if parity == 0 else near - far
        high = folded.astype(BF)
        low = (folded - high.astype(F32)).astype(BF)
        both = jnp.concatenate([high, low], axis=0)
        first = lax.dot_general(wave[parity], both, NT, preferred_element_type=F32)
        second = lax.dot_general(wave_lo[parity], high, NT, preferred_element_type=F32)
        halves.append(((first[:, :128] + first[:, 128:] + second) * SCALE).astype(BF))
    rows = []
    for c in range(2):
        at = slice(c * 512, c * 512 + 512)
        source = jnp.concatenate([halves[0][at], halves[1][at]], axis=0)
        rows.append(jnp.dot(chosen_t[...], source, preferred_element_type=F32).reshape(PARTS, 8, 128))
    out1[...] = jnp.concatenate(rows, axis=1).astype(BF)
    orders = Exchange(me, out1, in1, send_sems.at[1], recv1)
    orders.send_all()
    for load in leg_loads:
        load.wait()
    orders.wait_group(0, PARTS - 1)

    wide[...] = in1[...].astype(F32).reshape(2048, 128)
    blocks = []
    for o in range(8):
        for c in range(2):
            turned = wide[pl.ds(c * 8 + o, 128, stride=16), :].T
            blocks.append(jnp.concatenate([turned[i * F : (i + 1) * F] for i in range(8)], axis=1))
    spectra = jnp.dot(jnp.concatenate(blocks, axis=0).astype(BF), mix[...], preferred_element_type=F32)
    left[...] = (spectra * lat_ref[...]).astype(BF)

    def order(o, carry):
        at = pl.ds(aligned(o * 32, 32), 32)
        coefficients = lax.dot_general(left[at], leg[o], NT, preferred_element_type=F32)
        scaled = (coefficients * love_ref[...]).astype(BF)
        right[at] = jnp.dot(scaled, leg[o], preferred_element_type=F32).astype(BF)
        return carry

    lax.fori_loop(0, 8, order, 0)
    back = jnp.dot(right[...], mix_t[...], preferred_element_type=F32)
    for o in range(8):
        for c in range(2):
            block = back[(o * 2 + c) * F : (o * 2 + c + 1) * F]
            turned = jnp.concatenate([block[:, i * 128 : i * 128 + 128] for i in range(8)], axis=0).T
            wide[pl.ds(c * 8 + o, 128, stride=16), :] = turned
    out2[...] = wide[...].reshape(PACK).astype(BF)
    cycles = Exchange(me, out2, in2, send_sems.at[2], recv2)
    cycles.send_all()
    sums[...] = jnp.zeros_like(sums)
    cell_sums[...] = jnp.zeros_like(cell_sums)
    cycles.wait_group(0, PARTS - 1)

    arrived = in2[...].astype(F32)
    turned = []
    for c in range(2):
        source = arrived[:, c * 8 : c * 8 + 8].reshape(1024, 128).astype(BF)
        placed = jnp.dot(chosen[...], source, preferred_element_type=F32)
        turned.append(
            jnp.concatenate([placed[r * 128 : r * 128 + 128].T for r in range(8)], axis=1).astype(BF)
        )
    sides = []
    for parity in range(2):
        at = slice(parity * 512, parity * 512 + 512)
        source = jnp.concatenate([turned[0][:, at], turned[1][:, at]], axis=1)
        sides.append(
            jnp.dot(source, wave[parity], preferred_element_type=F32)
            + jnp.dot(source, wave_lo[parity], preferred_element_type=F32)
        )
    grid[:, :1024] = (sides[0] + sides[1]) * SCALE
    grid[:, 1024:] = (sides[0] - sides[1]) * SCALE

    def add_slots(b, carry):
        at = pl.ds(aligned(b * 1024, 1024), 1024)
        here = grid[pl.ds(aligned(b // 2 * F, F), F), pl.ds(aligned(b % 2 * 1024, 1024), 1024)]
        values, hots = [], []
        for k in range(3):
            row = sten_ref[k : k + 1, at]
            values.append(spread((here * wts_ref[k : k + 1, at]).astype(BF), row, 64))
            hots.append(lane_one_hot(row))
        sums[...] += lax.dot_general(
            jnp.concatenate(values, axis=1), jnp.concatenate(hots, axis=1), NT,
            preferred_element_type=F32,
        )
        return carry

    lax.fori_loop(0, 16, add_slots, 0)
    for g in range(64):
        out3[2 * g] = sums[g * F : (g + 1) * F, :128].astype(BF)
        out3[2 * g + 1] = sums[g * F : (g + 1) * F, 128:].astype(BF)
    home = Exchange(me, out3, in3, send_sems.at[3], recv3, 8)
    home.send_all()

    def add_cells(b):
        origins = [later(me, PARTS - (b * 8 + r)) for r in range(8)]
        row = jnp.concatenate([send_ref[0, pl.ds(q, 1), :] for q in origins], axis=1)
        values = jnp.concatenate([in3[q] for q in origins], axis=1)
        cell_sums[...] += lax.dot_general(
            spread(values, row, 32), lane_one_hot(row), NT, preferred_element_type=F32
        )

    home.wait_group(0, 7)
    add_cells(0)

    def next_cells(b, carry):
        home.wait_group(b, 8)
        add_cells(b)
        return carry

    lax.fori_loop(1, 16, next_cells, 0)
    for g in range(32):
        loading_ref[:, g * W : (g + 1) * W] = cell_sums[g * F : (g + 1) * F]
    for exchange in (cells, orders, cycles, home):
        exchange.wait_sent()


VM = pl.BlockSpec(memory_space=pltpu.VMEM)
ANY = pl.BlockSpec(memory_space=pl.ANY)


def shape(dims, kind=BF):
    return jax.ShapeDtypeStruct(dims, kind)


def waves():
    m = np.arange(1024)
    n = np.arange(1024)
    angle = 2.0 * math.pi * ((m[:, None] * n[None, :]) % 2048) / 2048.0
    table = np.stack([np.cos(angle), np.sin(angle)])
    table = np.stack([table[:, p::2].reshape(1024, 1024) for p in range(2)])
    high = table.astype(BF)
    return high, (table - high.astype(np.float64)).astype(BF)


def on_device(
    eta, forcing, couplings, neighbors, halo_send, cycle_send, stencil, stencil_weights,
    m_order, lat_weights, love, legendre,
):
    wave, wave_lo = (jnp.asarray(t) for t in waves())
    row = lambda x: x.reshape(1, -1)
    big = (2, 1024, 1024)
    return pl.pallas_call(
        kernel,
        out_shape=(shape(eta.shape, F32), shape(eta.shape, F32)),
        in_specs=[VM] * 6 + [ANY] * 2 + [VM] * 3 + [ANY] * 3,
        out_specs=(VM, VM),
        scratch_shapes=[
            pltpu.VMEM((34 * F, W), BF), pltpu.VMEM((32 * F, W), BF), pltpu.VMEM((F, 2 * W), BF),
            pltpu.VMEM((64 * F, W), BF), pltpu.VMEM((128, 2048), F32), pltpu.VMEM((2048, 128), F32),
            pltpu.VMEM((256, 1024), BF), pltpu.VMEM((256, 1024), BF),
            pltpu.VMEM((64 * F, W), F32), pltpu.VMEM((32 * F, W), F32),
        ]
        + [pltpu.VMEM((1024, 1024), BF)] * 4
        + [
            pltpu.VMEM(stencil.shape, I32), pltpu.VMEM(stencil.shape, F32),
            pltpu.VMEM(legendre.shape, BF), pltpu.VMEM(big, BF), pltpu.VMEM(big, BF),
        ]
        + [pltpu.VMEM(PACK, BF)] * 8
        + [pltpu.SemaphoreType.DMA((n,)) for n in (4, 8, 2, 2, 4, 1, 1, 1, 16)],
        compiler_params=pltpu.CompilerParams(
            collective_id=0, has_side_effects=True, vmem_limit_bytes=60 << 20
        ),
    )(
        eta, forcing, couplings, neighbors, halo_send, cycle_send, stencil, stencil_weights,
        row(m_order), row(lat_weights), row(love), legendre, wave, wave_lo,
    )


def solution(mesh):
    both = ("gx", "gy")
    cells = P(None, both)
    placed = (
        cells, cells, cells, cells, P(both, None), P(both, None, None), cells, cells,
        P(), P(), P(), P(both, None, None),
    )
    return jax.shard_map(
        on_device, mesh=mesh, in_specs=placed, out_specs=(cells, cells), check_vma=False
    )
```

```python
import functools
import math

import jax
import jax.numpy as jnp
import numpy as np
from jax import lax
from jax.experimental import pallas as pl
from jax.experimental.pallas import tpu as pltpu
from jax.sharding import PartitionSpec as P

BF = jnp.bfloat16
F32 = jnp.float32
I32 = jnp.int32
F = 16
W = 256
NT = (((1,), (1,)), ((), ()))
MESH = pl.DeviceIdType.MESH
AXES = ("gx", "gy")
PARTS = 128
PACK = (PARTS, F, 128)
SCALE = 2048.0**-0.5


def place(part):
    return (part // 16, lax.rem(part, 16))


def later(part, steps):
    return lax.rem(part + steps, PARTS)


class Exchange:
    def __init__(self, me, out, into, send_sem, recv_sems, group=PARTS):
        self.me, self.out, self.into = me, out, into
        self.send_sem, self.recv_sems, self.group = send_sem, recv_sems, group

    def send(self, steps):
        to = later(self.me, steps)
        pltpu.make_async_remote_copy(
            src_ref=self.out.at[to],
            dst_ref=self.into.at[self.me],
            send_sem=self.send_sem,
            recv_sem=self.recv_sems.at[steps // self.group],
            device_id=place(to),
            device_id_type=MESH,
        ).start()

    def keep(self):
        self.into[self.me] = self.out[self.me]

    def send_all(self):
        def one(steps, carry):
            self.send(steps)
            return carry

        lax.fori_loop(1, PARTS, one, 0)
        self.keep()

    def tiles(self, count, sem):
        at = pl.ds(0, count)
        return pltpu.make_async_remote_copy(
            src_ref=self.out.at[at],
            dst_ref=self.into.at[at],
            send_sem=self.send_sem,
            recv_sem=self.recv_sems.at[sem],
            device_id=place(later(self.me, 1)),
            device_id_type=MESH,
        )

    def wait_group(self, group, count):
        self.tiles(count, group).wait_recv()

    def wait_sent(self):
        self.tiles(PARTS - 1, 0).wait_send()


def as_rows(row):
    return jnp.broadcast_to(row.astype(F32), (F, row.shape[1])).astype(BF)


def marks(lanes, value):
    n = lanes.shape[1]
    rows = lax.broadcasted_iota(I32, (W, n), 0).astype(F32).astype(BF)
    tall = lambda x: jnp.concatenate([x] * (W // F), axis=0)
    return jnp.where(rows == tall(lanes), tall(value), BF(0))


def lane_one_hot(row):
    return marks(as_rows(row & (W - 1)), jnp.ones((F, row.shape[1]), BF))


def gather(table, row):
    n = row.shape[1]
    picked = jnp.dot(table, lane_one_hot(row), preferred_element_type=F32)
    group = jnp.broadcast_to(row >> 8, (F, n))
    out = jnp.zeros((F, n), F32)
    for g in range(table.shape[0] // F):
        out = jnp.where(group == g, picked[g * F : (g + 1) * F], out)
    return out


def spread(values, row, groups):
    group = as_rows(row >> 8)
    return jnp.concatenate(
        [jnp.where(group == BF(g), values, BF(0)) for g in range(groups)], axis=0
    )


def aligned(start, step):
    return pl.multiple_of(start, step)


def order_slot(row):
    return (row & 1) * 512 + (row >> 1)


def kernel(
    eta_ref, forcing_ref, coup_ref, nbr_ref, halo_ref, send_ref, sten_hbm, wts_hbm, m_ref, lat_ref,
    love_ref, leg_hbm, wave_hbm, wave_lo_hbm,
    stepped_ref, loading_ref,
    table, table2, rim, slots, grid, wide, left, right, sums, cell_sums, halo, turn, turn_t,
    sten_ref, wts_ref, leg, wave, wave_lo,
    out0, in0, out1, in1, out2, in2, out3, in3,
    load_sems, leg_sems, halo_send, halo_recv, send_sems, recv0, recv1, recv2, recv3,
):
    me = lax.axis_index("gx") * 16 + lax.axis_index("gy")
    barrier = pltpu.get_barrier_semaphore()

    def greet(steps, carry):
        pl.semaphore_signal(barrier, inc=1, device_id=place(later(me, steps)), device_id_type=MESH)
        return carry

    lax.fori_loop(1, PARTS, greet, 0)
    loads = [
        pltpu.make_async_copy(src, dst, load_sems.at[i])
        for i, (src, dst) in enumerate(
            [(sten_hbm, sten_ref), (wts_hbm, wts_ref), (wave_hbm, wave), (wave_lo_hbm, wave_lo)]
        )
    ]
    leg_loads = [pltpu.make_async_copy(leg_hbm.at[o], leg.at[o], leg_sems.at[o]) for o in range(8)]
    for load in loads:
        load.start()

    for g in range(32):
        table[g * F : (g + 1) * F] = eta_ref[:, g * W : (g + 1) * W].astype(BF)
    rim[...] = gather(table[...], halo_ref[...]).astype(BF)

    def step(b, carry):
        at = pl.ds(aligned(b * 1024, 1024), 1024)
        here = eta_ref[:, at]
        total = here + forcing_ref[:, at]
        sides = [None, None]
        for k in range(3):
            row = nbr_ref[k : k + 1, at]
            weight = coup_ref[k : k + 1, at]
            total += weight * (gather(table[...], row) - here)
            weights = jnp.broadcast_to(weight, (F, 1024)).astype(BF)
            for i in range(2):
                lanes = jnp.where(row >> 8 == 32 + i, row & (W - 1), -1)
                part = marks(as_rows(lanes), weights)
                sides[i] = part if k == 0 else sides[i] + part
        stepped_ref[:, at] = total
        for i in range(2):
            leg[b // 2, pl.ds(aligned(b % 2 * 512 + i * W, W), W)] = sides[i]
        return carry

    lax.fori_loop(0, 8, step, 0)

    pl.semaphore_wait(barrier, PARTS - 1)
    halos = []
    for i, (start, to) in enumerate([(W, later(me, 1)), (0, later(me, PARTS - 1))]):
        halos.append(
            pltpu.make_async_remote_copy(
                src_ref=rim.at[:, pl.ds(start, W)],
                dst_ref=halo.at[:, pl.ds(i * W, W)],
                send_sem=halo_send.at[i],
                recv_sem=halo_recv.at[i],
                device_id=place(to),
                device_id_type=MESH,
            )
        )
    for copy in halos:
        copy.start()
    slot = order_slot(m_ref[...])
    lane = lax.broadcasted_iota(I32, (128, 1024), 1)
    for r in range(8):
        at = slice(r * 128, r * 128 + 128)
        column = jnp.broadcast_to(slot[:, at].astype(F32), (128, 128)).T.astype(I32)
        for s in range(8):
            side = slice(s * 128, s * 128 + 128)
            turn[at, side] = jnp.where(column == lane[:, side], 1.0, 0.0).astype(BF)
    for copy in halos:
        copy.wait()
    for b in range(8):
        at = slice(b * 1024, b * 1024 + 1024)
        around = leg[b // 2, b % 2 * 512 : b % 2 * 512 + 512]
        total = stepped_ref[:, at] + jnp.dot(halo[...], around, preferred_element_type=F32)
        stepped_ref[:, at] = total
        rounded = total.astype(BF)
        for i in range(4):
            g = b * 4 + i
            table2[g * F : (g + 1) * F] = rounded[:, i * W : (i + 1) * W]
    for load in leg_loads:
        load.start()

    cells = Exchange(me, out0, in0, send_sems.at[0], recv0)

    def send(b, carry):
        steps = [b * 8 + r for r in range(8)]
        row = jnp.concatenate([send_ref[0, pl.ds(later(me, s), 1), :] for s in steps], axis=1)
        got = gather(table2[...], row).astype(BF)
        for r in range(8):
            out0[later(me, steps[r])] = got[:, r * 128 : r * 128 + 128]
            if r == 0:
                pl.when(b > 0)(functools.partial(cells.send, steps[r]))
            else:
                cells.send(steps[r])
        return carry

    lax.fori_loop(0, 16, send, 0)
    cells.keep()
    for load in loads:
        load.wait()
    cells.wait_group(0, PARTS - 1)
    for g in range(64):
        slots[g * F : (g + 1) * F, :128] = in0[2 * g]
        slots[g * F : (g + 1) * F, 128:] = in0[2 * g + 1]

    def pick(b, carry):
        at = pl.ds(aligned(b * 1024, 1024), 1024)
        total = jnp.zeros((F, 1024), F32)
        for k in range(3):
            total += gather(slots[...], sten_ref[k : k + 1, at]) * wts_ref[k : k + 1, at]
        grid[pl.ds(aligned(b // 2 * F, F), F), pl.ds(aligned(b % 2 * 1024, 1024), 1024)] = total
        return carry

    lax.fori_loop(0, 16, pick, 0, unroll=2)

    halves = []
    for parity in range(2):
        near, far = grid[:, :1024], grid[:, 1024:]
        folded = near + far if parity == 0 else near - far
        high = folded.astype(BF)
        low = (folded - high.astype(F32)).astype(BF)
        both = jnp.concatenate([high, low], axis=0)
        first = lax.dot_general(wave[parity], both, NT, preferred_element_type=F32)
        second = lax.dot_general(wave_lo[parity], high, NT, preferred_element_type=F32)
        halves.append(((first[:, :128] + first[:, 128:] + second) * SCALE).astype(BF))
    rows = []
    for c in range(2):
        at = slice(c * 512, c * 512 + 512)
        source = jnp.concatenate([halves[0][at], halves[1][at]], axis=0)
        rows.append(jnp.dot(turn[...], source, preferred_element_type=F32).reshape(PARTS, 8, 128))
    out1[...] = jnp.concatenate(rows, axis=1).astype(BF)
    orders = Exchange(me, out1, in1, send_sems.at[1], recv1)
    orders.send_all()
    for r in range(8):
        at = slice(r * 128, r * 128 + 128)
        row = lax.broadcasted_iota(I32, (128, 1024), 0) + r * 128
        turn[at] = jnp.where((lane >> 3) + (lane & 7) * 128 == row, 1.0, 0.0).astype(BF)
        turn_t[at] = jnp.where((row >> 3) + (row & 7) * 128 == lane, 1.0, 0.0).astype(BF)
    for load in leg_loads:
        load.wait()
    orders.wait_group(0, PARTS - 1)

    wide[...] = in1[...].astype(F32).reshape(2048, 128)
    blocks = []
    for o in range(8):
        for c in range(2):
            turned = wide[pl.ds(c * 8 + o, 128, stride=16), :].T
            blocks.append(jnp.concatenate([turned[i * F : (i + 1) * F] for i in range(8)], axis=1))
    spectra = jnp.dot(jnp.concatenate(blocks, axis=0).astype(BF), turn[...], preferred_element_type=F32)
    left[...] = (spectra * lat_ref[...]).astype(BF)

    def order(o, carry):
        at = pl.ds(aligned(o * 32, 32), 32)
        coefficients = lax.dot_general(left[at], leg[o], NT, preferred_element_type=F32)
        scaled = (coefficients * love_ref[...]).astype(BF)
        right[at] = jnp.dot(scaled, leg[o], preferred_element_type=F32).astype(BF)
        return carry

    lax.fori_loop(0, 8, order, 0, unroll=4)
    back = jnp.dot(right[...], turn_t[...], preferred_element_type=F32)
    for o in range(8):
        for c in range(2):
            block = back[(o * 2 + c) * F : (o * 2 + c + 1) * F]
            turned = jnp.concatenate([block[:, i * 128 : i * 128 + 128] for i in range(8)], axis=0).T
            wide[pl.ds(c * 8 + o, 128, stride=16), :] = turned
    out2[...] = wide[...].reshape(PACK).astype(BF)
    cycles = Exchange(me, out2, in2, send_sems.at[2], recv2)
    cycles.send_all()
    for r in range(8):
        row = lax.broadcasted_iota(I32, (128, 1024), 0) + r * 128
        turn[r * 128 : r * 128 + 128] = jnp.where(slot == row, 1.0, 0.0).astype(BF)
    sums[...] = jnp.zeros_like(sums)
    cell_sums[...] = jnp.zeros_like(cell_sums)
    cycles.wait_group(0, PARTS - 1)

    arrived = in2[...].astype(F32)
    turned = []
    for c in range(2):
        source = arrived[:, c * 8 : c * 8 + 8].reshape(1024, 128).astype(BF)
        placed = jnp.dot(turn[...], source, preferred_element_type=F32)
        turned.append(
            jnp.concatenate([placed[r * 128 : r * 128 + 128].T for r in range(8)], axis=1).astype(BF)
        )
    sides = []
    for parity in range(2):
        at = slice(parity * 512, parity * 512 + 512)
        source = jnp.concatenate([turned[0][:, at], turned[1][:, at]], axis=1)
        sides.append(
            jnp.dot(source, wave[parity], preferred_element_type=F32)
            + jnp.dot(source, wave_lo[parity], preferred_element_type=F32)
        )
    grid[:, :1024] = (sides[0] + sides[1]) * SCALE
    grid[:, 1024:] = (sides[0] - sides[1]) * SCALE

    def add_slots(b, carry):
        at = pl.ds(aligned(b * 2048, 2048), 2048)
        here = grid[pl.ds(aligned(b * F, F), F), :]
        values, hots = [], []
        for k in range(3):
            row = sten_ref[k : k + 1, at]
            values.append(spread((here * wts_ref[k : k + 1, at]).astype(BF), row, 64))
            hots.append(lane_one_hot(row))
        sums[...] += lax.dot_general(
            jnp.concatenate(values, axis=1), jnp.concatenate(hots, axis=1), NT,
            preferred_element_type=F32,
        )
        return carry

    lax.fori_loop(0, 8, add_slots, 0)
    for g in range(64):
        out3[2 * g] = sums[g * F : (g + 1) * F, :128].astype(BF)
        out3[2 * g + 1] = sums[g * F : (g + 1) * F, 128:].astype(BF)
    home = Exchange(me, out3, in3, send_sems.at[3], recv3, 8)
    home.send_all()

    def add_cells(b):
        origins = [later(me, PARTS - (b * 8 + r)) for r in range(8)]
        row = jnp.concatenate([send_ref[0, pl.ds(q, 1), :] for q in origins], axis=1)
        values = jnp.concatenate([in3[q] for q in origins], axis=1)
        cell_sums[...] += lax.dot_general(
            spread(values, row, 32), lane_one_hot(row), NT, preferred_element_type=F32
        )

    home.wait_group(0, 7)
    add_cells(0)

    def next_cells(b, carry):
        home.wait_group(b, 8)
        add_cells(b)
        return carry

    lax.fori_loop(1, 16, next_cells, 0)
    for g in range(32):
        loading_ref[:, g * W : (g + 1) * W] = cell_sums[g * F : (g + 1) * F]
    for exchange in (cells, orders, cycles, home):
        exchange.wait_sent()


VM = pl.BlockSpec(memory_space=pltpu.VMEM)
ANY = pl.BlockSpec(memory_space=pl.ANY)


def shape(dims, kind=BF):
    return jax.ShapeDtypeStruct(dims, kind)


def waves():
    m = np.arange(1024)
    n = np.arange(1024)
    angle = 2.0 * math.pi * ((m[:, None] * n[None, :]) % 2048) / 2048.0
    table = np.stack([np.cos(angle), np.sin(angle)])
    table = np.stack([table[:, p::2].reshape(1024, 1024) for p in range(2)])
    high = table.astype(BF)
    return high, (table - high.astype(np.float64)).astype(BF)


def on_device(
    eta, forcing, couplings, neighbors, halo_send, cycle_send, stencil, stencil_weights,
    m_order, lat_weights, love, legendre,
):
    wave, wave_lo = (jnp.asarray(t) for t in waves())
    row = lambda x: x.reshape(1, -1)
    big = (2, 1024, 1024)
    return pl.pallas_call(
        kernel,
        out_shape=(shape(eta.shape, F32), shape(eta.shape, F32)),
        in_specs=[VM] * 6 + [ANY] * 2 + [VM] * 3 + [ANY] * 3,
        out_specs=(VM, VM),
        scratch_shapes=[
            pltpu.VMEM((32 * F, W), BF), pltpu.VMEM((32 * F, W), BF), pltpu.VMEM((F, 2 * W), BF),
            pltpu.VMEM((64 * F, W), BF), pltpu.VMEM((128, 2048), F32), pltpu.VMEM((2048, 128), F32),
            pltpu.VMEM((256, 1024), BF), pltpu.VMEM((256, 1024), BF),
            pltpu.VMEM((64 * F, W), F32), pltpu.VMEM((32 * F, W), F32),
        ]
        + [pltpu.VMEM((F, 2 * W), BF), pltpu.VMEM((1024, 1024), BF), pltpu.VMEM((1024, 1024), BF)]
        + [
            pltpu.VMEM(stencil.shape, I32), pltpu.VMEM(stencil.shape, F32),
            pltpu.VMEM(legendre.shape, BF), pltpu.VMEM(big, BF), pltpu.VMEM(big, BF),
        ]
        + [pltpu.VMEM(PACK, BF)] * 8
        + [pltpu.SemaphoreType.DMA((n,)) for n in (4, 8, 2, 2, 4, 1, 1, 1, 16)],
        compiler_params=pltpu.CompilerParams(
            collective_id=0, has_side_effects=True, vmem_limit_bytes=60 << 20
        ),
    )(
        eta, forcing, couplings, neighbors, halo_send, cycle_send, stencil, stencil_weights,
        row(m_order), row(lat_weights), row(love), legendre, wave, wave_lo,
    )
def solution(mesh):
    both = ("gx", "gy")
    cells = P(None, both)
    placed = (
        cells, cells, cells, cells, P(both, None), P(both, None, None), cells, cells,
        P(), P(), P(), P(both, None, None),
    )
    return jax.shard_map(
        on_device, mesh=mesh, in_specs=placed, out_specs=(cells, cells), check_vma=False
    )
```

```python
import functools
import math

import jax
import jax.numpy as jnp
import numpy as np
from jax import lax
from jax.experimental import pallas as pl
from jax.experimental.pallas import tpu as pltpu
from jax.sharding import PartitionSpec as P

BF = jnp.bfloat16
F32 = jnp.float32
I32 = jnp.int32
F = 16
W = 256
NT = (((1,), (1,)), ((), ()))
MESH = pl.DeviceIdType.MESH
AXES = ("gx", "gy")
PARTS = 128
PACK = (PARTS, F, 128)
SCALE = 2048.0**-0.5


def place(part):
    return (part // 16, lax.rem(part, 16))


def later(part, steps):
    return lax.rem(part + steps, PARTS)


class Exchange:
    def __init__(self, me, out, into, send_sem, recv_sems, group=PARTS):
        self.me, self.out, self.into = me, out, into
        self.send_sem, self.recv_sems, self.group = send_sem, recv_sems, group

    def send(self, steps):
        to = later(self.me, steps)
        pltpu.make_async_remote_copy(
            src_ref=self.out.at[to],
            dst_ref=self.into.at[self.me],
            send_sem=self.send_sem,
            recv_sem=self.recv_sems.at[steps // self.group],
            device_id=place(to),
            device_id_type=MESH,
        ).start()

    def keep(self):
        self.into[self.me] = self.out[self.me]

    def send_range(self, first, end):
        def one(steps, carry):
            self.send(steps)
            return carry

        lax.fori_loop(first, end, one, 0)

    def send_all(self):
        self.send_range(1, PARTS)
        self.keep()

    def tiles(self, count, sem):
        at = pl.ds(0, count)
        return pltpu.make_async_remote_copy(
            src_ref=self.out.at[at],
            dst_ref=self.into.at[at],
            send_sem=self.send_sem,
            recv_sem=self.recv_sems.at[sem],
            device_id=place(later(self.me, 1)),
            device_id_type=MESH,
        )

    def wait_group(self, group, count):
        self.tiles(count, group).wait_recv()

    def wait_sent(self):
        self.tiles(PARTS - 1, 0).wait_send()


def as_rows(row):
    return jnp.broadcast_to(row.astype(F32), (F, row.shape[1])).astype(BF)


def marks(lanes, value):
    n = lanes.shape[1]
    rows = lax.broadcasted_iota(I32, (W, n), 0).astype(F32).astype(BF)
    tall = lambda x: jnp.concatenate([x] * (W // F), axis=0)
    return jnp.where(rows == tall(lanes), tall(value), BF(0))


def lane_one_hot(row):
    return marks(as_rows(row & (W - 1)), jnp.ones((F, row.shape[1]), BF))


def gather(table, row):
    n = row.shape[1]
    picked = jnp.dot(table, lane_one_hot(row), preferred_element_type=F32)
    group = jnp.broadcast_to(row >> 8, (F, n))
    out = jnp.zeros((F, n), F32)
    for g in range(table.shape[0] // F):
        out = jnp.where(group == g, picked[g * F : (g + 1) * F], out)
    return out


def spread(values, row, groups):
    group = as_rows(row >> 8)
    return jnp.concatenate(
        [jnp.where(group == BF(g), values, BF(0)) for g in range(groups)], axis=0
    )


def aligned(start, step):
    return pl.multiple_of(start, step)


def order_slot(row):
    return (row & 1) * 512 + (row >> 1)


def kernel(
    eta_ref, forcing_ref, coup_ref, nbr_ref, halo_ref, send_ref, sten_hbm, wts_hbm, m_ref, lat_ref,
    love_ref, leg_hbm, wave_hbm, wave_lo_hbm,
    stepped_ref, loading_ref,
    table, table2, rim, slots, grid, wide, left, right, sums, cell_sums, halo, turn, turn_t,
    sten_ref, wts_ref, leg, wave, wave_lo,
    out0, in0, out1, in1, out2, in2, out3, in3,
    load_sems, leg_sems, halo_send, halo_recv, send_sems, recv0, recv1, recv2, recv3,
):
    me = lax.axis_index("gx") * 16 + lax.axis_index("gy")
    barrier = pltpu.get_barrier_semaphore()

    def greet(steps, carry):
        pl.semaphore_signal(barrier, inc=1, device_id=place(later(me, steps)), device_id_type=MESH)
        return carry

    lax.fori_loop(1, PARTS, greet, 0)
    loads = [
        pltpu.make_async_copy(src, dst, load_sems.at[i])
        for i, (src, dst) in enumerate(
            [(sten_hbm, sten_ref), (wts_hbm, wts_ref), (wave_hbm, wave), (wave_lo_hbm, wave_lo)]
        )
    ]
    leg_loads = [pltpu.make_async_copy(leg_hbm.at[o], leg.at[o], leg_sems.at[o]) for o in range(8)]
    for load in loads:
        load.start()

    for g in range(32):
        table[g * F : (g + 1) * F] = eta_ref[:, g * W : (g + 1) * W].astype(BF)
    rim[...] = gather(table[...], halo_ref[...]).astype(BF)

    def step(b, carry):
        at = pl.ds(aligned(b * 1024, 1024), 1024)
        here = eta_ref[:, at]
        total = here + forcing_ref[:, at]
        sides = [None, None]
        for k in range(3):
            row = nbr_ref[k : k + 1, at]
            weight = coup_ref[k : k + 1, at]
            total += weight * (gather(table[...], row) - here)
            weights = jnp.broadcast_to(weight, (F, 1024)).astype(BF)
            for i in range(2):
                lanes = jnp.where(row >> 8 == 32 + i, row & (W - 1), -1)
                part = marks(as_rows(lanes), weights)
                sides[i] = part if k == 0 else sides[i] + part
        stepped_ref[:, at] = total
        for i in range(2):
            leg[b // 2, pl.ds(aligned(b % 2 * 512 + i * W, W), W)] = sides[i]
        return carry

    lax.fori_loop(0, 8, step, 0)

    pl.semaphore_wait(barrier, PARTS - 1)
    halos = []
    for i, (start, to) in enumerate([(W, later(me, 1)), (0, later(me, PARTS - 1))]):
        halos.append(
            pltpu.make_async_remote_copy(
                src_ref=rim.at[:, pl.ds(start, W)],
                dst_ref=halo.at[:, pl.ds(i * W, W)],
                send_sem=halo_send.at[i],
                recv_sem=halo_recv.at[i],
                device_id=place(to),
                device_id_type=MESH,
            )
        )
    for copy in halos:
        copy.start()
    slot = order_slot(m_ref[...])
    lane = lax.broadcasted_iota(I32, (128, 1024), 1)
    for r in range(8):
        at = slice(r * 128, r * 128 + 128)
        column = jnp.broadcast_to(slot[:, at].astype(F32), (128, 128)).T.astype(I32)
        for s in range(8):
            side = slice(s * 128, s * 128 + 128)
            turn[at, side] = jnp.where(column == lane[:, side], 1.0, 0.0).astype(BF)
    for copy in halos:
        copy.wait()
    for b in range(8):
        at = slice(b * 1024, b * 1024 + 1024)
        around = leg[b // 2, b % 2 * 512 : b % 2 * 512 + 512]
        total = stepped_ref[:, at] + jnp.dot(halo[...], around, preferred_element_type=F32)
        stepped_ref[:, at] = total
        rounded = total.astype(BF)
        for i in range(4):
            g = b * 4 + i
            table2[g * F : (g + 1) * F] = rounded[:, i * W : (i + 1) * W]
    for load in leg_loads:
        load.start()

    cells = Exchange(me, out0, in0, send_sems.at[0], recv0, PARTS // 2)

    def send(b, carry):
        steps = [b * 8 + r for r in range(8)]
        row = jnp.concatenate([send_ref[0, pl.ds(later(me, s), 1), :] for s in steps], axis=1)
        got = gather(table2[...], row).astype(BF)
        for r in range(8):
            out0[later(me, steps[r])] = got[:, r * 128 : r * 128 + 128]
            if r == 0:
                pl.when(b > 0)(functools.partial(cells.send, steps[r]))
            else:
                cells.send(steps[r])
        return carry

    lax.fori_loop(0, 16, send, 0)
    cells.keep()
    for load in loads:
        load.wait()

    for half in range(2):
        cells.wait_group(half, 63 + half)
        for g in range(32 * half, 32 * half + 32):
            slots[g * F : (g + 1) * F, :128] = in0[later(me, PARTS - 2 * g)]
            slots[g * F : (g + 1) * F, 128:] = in0[later(me, PARTS - 2 * g - 1)]

        def pick(b, carry):
            at = pl.ds(aligned(b * 2048, 2048), 2048)
            into = pl.ds(aligned(b * F, F), F)
            total = jnp.zeros((F, 2048), F32) if half == 0 else grid[into, :]
            for k in range(3):
                row = sten_ref[k : k + 1, at]
                below = (me - (row >> 7) + PARTS) & (PARTS - 1)
                row = (below << 7) + (row & 127) - half * 8192
                total += gather(slots[half * 512 : half * 512 + 512], row) * wts_ref[k : k + 1, at]
            grid[into, :] = total
            return carry

        lax.fori_loop(0, 8, pick, 0)

    halves = []
    for parity in range(2):
        near, far = grid[:, :1024], grid[:, 1024:]
        folded = near + far if parity == 0 else near - far
        high = folded.astype(BF)
        low = (folded - high.astype(F32)).astype(BF)
        both = jnp.concatenate([high, low], axis=0)
        first = lax.dot_general(wave[parity], both, NT, preferred_element_type=F32)
        second = lax.dot_general(wave_lo[parity], high, NT, preferred_element_type=F32)
        halves.append(((first[:, :128] + first[:, 128:] + second) * SCALE).astype(BF))
    rows = []
    for c in range(2):
        at = slice(c * 512, c * 512 + 512)
        source = jnp.concatenate([halves[0][at], halves[1][at]], axis=0)
        rows.append(jnp.dot(turn[...], source, preferred_element_type=F32).reshape(PARTS, 8, 128))
    out1[...] = jnp.concatenate(rows, axis=1).astype(BF)
    orders = Exchange(me, out1, in1, send_sems.at[1], recv1)
    orders.send_all()
    for r in range(8):
        at = slice(r * 128, r * 128 + 128)
        row = lax.broadcasted_iota(I32, (128, 1024), 0) + r * 128
        turn[at] = jnp.where((lane >> 3) + (lane & 7) * 128 == row, 1.0, 0.0).astype(BF)
        turn_t[at] = jnp.where((row >> 3) + (row & 7) * 128 == lane, 1.0, 0.0).astype(BF)
    for load in leg_loads:
        load.wait()
    orders.wait_group(0, PARTS - 1)

    wide[...] = in1[...].astype(F32).reshape(2048, 128)
    blocks = []
    for o in range(8):
        for c in range(2):
            turned = wide[pl.ds(c * 8 + o, 128, stride=16), :].T
            blocks.append(jnp.concatenate([turned[i * F : (i + 1) * F] for i in range(8)], axis=1))
    spectra = jnp.dot(jnp.concatenate(blocks, axis=0).astype(BF), turn[...], preferred_element_type=F32)
    left[...] = (spectra * lat_ref[...]).astype(BF)

    def order(o, carry):
        at = pl.ds(aligned(o * 32, 32), 32)
        coefficients = lax.dot_general(left[at], leg[o], NT, preferred_element_type=F32)
        scaled = (coefficients * love_ref[...]).astype(BF)
        right[at] = jnp.dot(scaled, leg[o], preferred_element_type=F32).astype(BF)
        return carry

    lax.fori_loop(0, 8, order, 0, unroll=4)
    back = jnp.dot(right[...], turn_t[...], preferred_element_type=F32)
    for o in range(8):
        for c in range(2):
            block = back[(o * 2 + c) * F : (o * 2 + c + 1) * F]
            turned = jnp.concatenate([block[:, i * 128 : i * 128 + 128] for i in range(8)], axis=0).T
            wide[pl.ds(c * 8 + o, 128, stride=16), :] = turned
    out2[...] = wide[...].reshape(PACK).astype(BF)
    cycles = Exchange(me, out2, in2, send_sems.at[2], recv2)
    cycles.send_all()
    for r in range(8):
        row = lax.broadcasted_iota(I32, (128, 1024), 0) + r * 128
        turn[r * 128 : r * 128 + 128] = jnp.where(slot == row, 1.0, 0.0).astype(BF)
    sums[...] = jnp.zeros_like(sums)
    cell_sums[...] = jnp.zeros_like(cell_sums)
    cycles.wait_group(0, PARTS - 1)

    arrived = in2[...].astype(F32)
    turned = []
    for c in range(2):
        source = arrived[:, c * 8 : c * 8 + 8].reshape(1024, 128).astype(BF)
        placed = jnp.dot(turn[...], source, preferred_element_type=F32)
        turned.append(
            jnp.concatenate([placed[r * 128 : r * 128 + 128].T for r in range(8)], axis=1).astype(BF)
        )
    sides = []
    for parity in range(2):
        at = slice(parity * 512, parity * 512 + 512)
        source = jnp.concatenate([turned[0][:, at], turned[1][:, at]], axis=1)
        sides.append(
            jnp.dot(source, wave[parity], preferred_element_type=F32)
            + jnp.dot(source, wave_lo[parity], preferred_element_type=F32)
        )
    grid[:, :1024] = (sides[0] + sides[1]) * SCALE
    grid[:, 1024:] = (sides[0] - sides[1]) * SCALE

    home = Exchange(me, out3, in3, send_sems.at[3], recv3, 8)
    for half in range(2):
        rows = slice(half * 512, half * 512 + 512)

        def add_slots(b, carry):
            at = pl.ds(aligned(b * 2048, 2048), 2048)
            here = grid[pl.ds(aligned(b * F, F), F), :]
            values, hots = [], []
            for k in range(3):
                row = sten_ref[k : k + 1, at]
                above = ((row >> 7) - me + PARTS) & (PARTS - 1)
                row = (above << 7) + (row & 127) - half * 8192
                values.append(spread((here * wts_ref[k : k + 1, at]).astype(BF), row, 32))
                hots.append(lane_one_hot(row))
            sums[rows] += lax.dot_general(
                jnp.concatenate(values, axis=1), jnp.concatenate(hots, axis=1), NT,
                preferred_element_type=F32,
            )
            return carry

        lax.fori_loop(0, 8, add_slots, 0)
        for g in range(32 * half, 32 * half + 32):
            out3[later(me, 2 * g)] = sums[g * F : (g + 1) * F, :128].astype(BF)
            out3[later(me, 2 * g + 1)] = sums[g * F : (g + 1) * F, 128:].astype(BF)
        home.send_range(max(half * 64, 1), half * 64 + 64)
    home.keep()

    def add_cells(b):
        origins = [later(me, PARTS - (b * 8 + r)) for r in range(8)]
        row = jnp.concatenate([send_ref[0, pl.ds(q, 1), :] for q in origins], axis=1)
        values = jnp.concatenate([in3[q] for q in origins], axis=1)
        cell_sums[...] += lax.dot_general(
            spread(values, row, 32), lane_one_hot(row), NT, preferred_element_type=F32
        )

    home.wait_group(0, 7)
    add_cells(0)

    def next_cells(b, carry):
        home.wait_group(b, 8)
        add_cells(b)
        return carry

    lax.fori_loop(1, 16, next_cells, 0)
    for g in range(32):
        loading_ref[:, g * W : (g + 1) * W] = cell_sums[g * F : (g + 1) * F]
    for exchange in (cells, orders, cycles, home):
        exchange.wait_sent()


VM = pl.BlockSpec(memory_space=pltpu.VMEM)
ANY = pl.BlockSpec(memory_space=pl.ANY)


def shape(dims, kind=BF):
    return jax.ShapeDtypeStruct(dims, kind)


def waves():
    m = np.arange(1024)
    n = np.arange(1024)
    angle = 2.0 * math.pi * ((m[:, None] * n[None, :]) % 2048) / 2048.0
    table = np.stack([np.cos(angle), np.sin(angle)])
    table = np.stack([table[:, p::2].reshape(1024, 1024) for p in range(2)])
    high = table.astype(BF)
    return high, (table - high.astype(np.float64)).astype(BF)


def on_device(
    eta, forcing, couplings, neighbors, halo_send, cycle_send, stencil, stencil_weights,
    m_order, lat_weights, love, legendre,
):
    wave, wave_lo = (jnp.asarray(t) for t in waves())
    row = lambda x: x.reshape(1, -1)
    big = (2, 1024, 1024)
    return pl.pallas_call(
        kernel,
        out_shape=(shape(eta.shape, F32), shape(eta.shape, F32)),
        in_specs=[VM] * 6 + [ANY] * 2 + [VM] * 3 + [ANY] * 3,
        out_specs=(VM, VM),
        scratch_shapes=[
            pltpu.VMEM((32 * F, W), BF), pltpu.VMEM((32 * F, W), BF), pltpu.VMEM((F, 2 * W), BF),
            pltpu.VMEM((64 * F, W), BF), pltpu.VMEM((128, 2048), F32), pltpu.VMEM((2048, 128), F32),
            pltpu.VMEM((256, 1024), BF), pltpu.VMEM((256, 1024), BF),
            pltpu.VMEM((64 * F, W), F32), pltpu.VMEM((32 * F, W), F32),
        ]
        + [pltpu.VMEM((F, 2 * W), BF), pltpu.VMEM((1024, 1024), BF), pltpu.VMEM((1024, 1024), BF)]
        + [
            pltpu.VMEM(stencil.shape, I32), pltpu.VMEM(stencil.shape, F32),
            pltpu.VMEM(legendre.shape, BF), pltpu.VMEM(big, BF), pltpu.VMEM(big, BF),
        ]
        + [pltpu.VMEM(PACK, BF)] * 8
        + [pltpu.SemaphoreType.DMA((n,)) for n in (4, 8, 2, 2, 4, 2, 1, 1, 16)],
        compiler_params=pltpu.CompilerParams(
            collective_id=0, has_side_effects=True, vmem_limit_bytes=60 << 20
        ),
    )(
        eta, forcing, couplings, neighbors, halo_send, cycle_send, stencil, stencil_weights,
        row(m_order), row(lat_weights), row(love), legendre, wave, wave_lo,
    )
def solution(mesh):
    both = ("gx", "gy")
    cells = P(None, both)
    placed = (
        cells, cells, cells, cells, P(both, None), P(both, None, None), cells, cells,
        P(), P(), P(), P(both, None, None),
    )
    return jax.shard_map(
        on_device, mesh=mesh, in_specs=placed, out_specs=(cells, cells), check_vma=False
    )
```
